32 devices in a mesh: seq: 8 (over z, x), heads: 4 (over y, core).
Axes of the slice: x: 2, y: 2, z: 4, core: 2. Of those that a mesh axis runs over, the one named last changes fastest.
Arguments:
- audio: bfloat16 [2048, 1280], P('seq'), may hold values from -6 to 6
- ln_gain: float32 [1280], replicated, may hold values from 0.25 to 1.75
- ln_shift: float32 [1280], replicated, may hold values from -3 to 3
- enc_wq: bfloat16 [1280, 1024], P(None, 'heads'), may hold values from -0.15625 to 0.15625
- enc_bq: float32 [1024], P('heads'), may hold values from -3 to 3
- enc_wk: bfloat16 [1280, 1024], P(None, 'heads'), may hold values from -4 to 4
- enc_wv: bfloat16 [1280, 1024], P(None, 'heads'), may hold values from -0.15625 to 0.15625
- enc_bv: float32 [1024], P('heads'), may hold values from -3 to 3
- enc_wo: bfloat16 [1024, 1280], P('heads'), may hold values from -0.1875 to 0.1875
- enc_bo: float32 [1280], replicated, may hold values from -3 to 3
- windows: int32 [16], P('heads'), may hold values from 1 to 128, as said below
- dec_wkv: bfloat16 [1280, 8, 256], replicated, may hold values from -4 to 4
- dec_bv: float32 [8, 128], replicated, may hold values from -3 to 3
- text: bfloat16 [4096, 8192], P('seq'), may hold values from -6 to 6
- norm_gain: float32 [8192], replicated, may hold values from 0.25 to 1.75
- dec_wq: bfloat16 [8192, 4096], P('seq', 'heads'), may hold values from -0.0625 to 0.0625
- dec_bq: float32 [4096], P('heads'), may hold values from -3 to 3
- dec_wo: bfloat16 [4096, 8192], P('heads', 'seq'), may hold values from -0.125 to 0.125
- span_start: int32 [4096], P('seq'), may hold values from 0 to 1792, as said below
- span_len: int32 [4096], P('seq'), may hold values from 1 to 256, as said below
Outputs:
- enc_out: bfloat16 [2048, 1280], P(('seq', 'heads'))
- dec_out: bfloat16 [4096, 8192], P('seq', 'heads')
The draws below stay inside these ranges and needn't reach their ends.
Inputs may be any that keep to these rules, and one draw needn't show every extreme that they name: `windows`: every head's window is 1 to 128; some head has exactly 128 and some head exactly 1. `span_start`: row r's band begins between r * 256 // 512 - 255 and r * 256 // 512, and never before frame 0 or after 2048 - 256; row 0 begins at 0 and the last row at 1792; the last row of every aligned block of 512 rows but the final one begins exactly at r * 256 // 512. `span_len`: row 0 has 256 valid frames and row 1 has one; the last row of every aligned block of 512 rows has 256, unless it is row 1.
All inputs are finite; a program needn't handle non-finite values.
Results may differ from the reference program's by a relative error of at most 0.025.
Values may be sent and summed in bfloat16 or wider, within the bound.
A program may use at most 128 MiB of HBM per device.

```python
import jax
import jax.numpy as jnp
from jax import lax

D_ENC = 1280
EH = 16
EHD = 64
EWIN = 128
FR_SEQ = 256
FRAMES = 2048
D = 8192
KVG = 8
QPG = 4
HD = 128
GL = 2
BAND = 256
ROWS_DEV = 512
ROWS = 4096
N_SEQ = 8
N_HEADS = 4


def draw_windows(key, part):
    key_one, key_two = jax.random.split(key)
    widths = jax.random.randint(key_one, (EH,), 1, EWIN + 1, dtype=jnp.int32)
    shuffled = jax.random.permutation(key_two, EH)
    return widths.at[shuffled[0]].set(EWIN).at[shuffled[1]].set(1)


def draw_span_start(key, part):
    row_ids = jnp.arange(ROWS, dtype=jnp.int32)
    centres = row_ids * FR_SEQ // ROWS_DEV
    offsets = jax.random.randint(key, (ROWS,), 0, BAND, dtype=jnp.int32)
    block_last = row_ids % ROWS_DEV == ROWS_DEV - 1
    offsets = jnp.where(block_last, jnp.zeros_like(offsets), offsets)
    begins = jnp.clip(centres - offsets, 0, FRAMES - BAND)
    return begins.at[ROWS - 1].set(FRAMES - BAND)


def draw_span_len(key, part):
    row_ids = jnp.arange(ROWS, dtype=jnp.int32)
    counts = jax.random.randint(key, (ROWS,), 1, BAND + 1, dtype=jnp.int32)
    block_last = row_ids % ROWS_DEV == ROWS_DEV - 1
    counts = jnp.where(block_last, jnp.full_like(counts, BAND), counts)
    return counts.at[0].set(BAND).at[1].set(1)


def shift_values(key):
    return 0.5 * jax.random.truncated_normal(jax.random.fold_in(key, 101), -6.0, 6.0, (D_ENC,), jnp.float32)


def output_bias_values(key):
    return 0.5 * jax.random.truncated_normal(jax.random.fold_in(key, 201), -6.0, 6.0, (D_ENC,), jnp.float32)


def draw_audio(key, part):
    values = jax.random.truncated_normal(jax.random.fold_in(key, 301), -6.0, 6.0, (FRAMES, D_ENC), jnp.float32)
    return values.astype(jnp.bfloat16)


def draw_ln_shift(key, part):
    return shift_values(key)


def draw_enc_bo(key, part):
    return output_bias_values(key)


def draw_enc_wk(key, part):
    column_count = EH * EHD
    base_draw = jax.random.truncated_normal(jax.random.fold_in(key, 102), -6.0, 6.0, (D_ENC, column_count), jnp.float32) * D_ENC ** (-0.5)
    return base_draw.astype(jnp.bfloat16)


def draw_dec_wkv(key, part):
    base_draw = jax.random.truncated_normal(jax.random.fold_in(key, 202), -6.0, 6.0, (D_ENC, KVG, 2 * HD), jnp.float32) * D_ENC ** (-0.5)
    return base_draw.astype(jnp.bfloat16)


def strengthened(result, own_key, source, target, blocks, factor):
    owner, partner = [(jnp.arange(result.shape[position]) // (result.shape[position] // blocks)).reshape([-1 if axis == position else 1 for axis in range(result.ndim)]) for position in (source, target)]
    chosen = jax.random.permutation(own_key, blocks)[partner]
    strong = (owner == chosen) | (owner == (partner + blocks // 2) % blocks)
    return jnp.where(strong, factor * result, result)


def block_scale(key, shape, pieces, least, top_value):
    factor_of, own = 1.0, jax.random.fold_in(key, 6)
    for position, parts in pieces:
        steps = jnp.exp(jax.random.uniform(jax.random.fold_in(own, position), (parts,), jnp.float32, least / len(pieces), top_value / len(pieces)))
        factor_of = factor_of * jnp.repeat(steps, shape[position] // parts).reshape([-1 if axis == position else 1 for axis in range(len(shape))])
    return factor_of


def normal_values(rng, dims, scale, bound, cuts=(), held_as=jnp.bfloat16):
    factor_of = block_scale(rng, dims, cuts, -0.22, 0.18) if cuts else 1.0
    result = jax.random.normal(rng, dims, jnp.float32) * scale * factor_of
    return jnp.minimum(jnp.maximum(result, -bound), bound).astype(held_as)


def heavy_noise(own_key, dims, deviation, limit, pieces, heavy, kind=jnp.bfloat16):
    result = deviation * jax.random.normal(own_key, dims, jnp.float32)
    if pieces:
        result = result * block_scale(own_key, dims, pieces, -0.22, 0.18)
    return jnp.clip(strengthened(result, jax.random.fold_in(own_key, 3), *heavy), -limit, limit).astype(kind)


def setup_inputs(seed: int = 0) -> dict:
    arg_keys = jax.random.split(jax.random.key(seed), 21)
    audio = draw_audio(jax.random.fold_in(arg_keys[20], 71), 0)
    ln_gain = jnp.clip(1.0 + 0.15 * jax.random.normal(arg_keys[1], (D_ENC,), jnp.float32), 0.25, 1.75)
    ln_shift = draw_ln_shift(jax.random.fold_in(arg_keys[20], 71), 0)
    enc_wq = normal_values(arg_keys[3], (D_ENC, EH * EHD), D_ENC ** -0.5, 0.15625, ((1, 4),))
    enc_bq = normal_values(arg_keys[4], (EH * EHD,), 0.5, 3.0, ((0, 4),), jnp.float32)
    enc_wk = draw_enc_wk(jax.random.fold_in(arg_keys[20], 71), 0)
    enc_wv = normal_values(arg_keys[6], (D_ENC, EH * EHD), D_ENC ** -0.5, 0.15625, ((1, 4),))
    enc_bv = normal_values(arg_keys[7], (EH * EHD,), 0.5, 3.0, ((0, 4),), jnp.float32)
    enc_wo = normal_values(arg_keys[8], (EH * EHD, D_ENC), (EH * EHD) ** -0.5, 0.1875, ((0, 4),))
    enc_bo = draw_enc_bo(jax.random.fold_in(arg_keys[20], 71), 0)
    windows = draw_windows(jax.random.fold_in(arg_keys[20], 71), 0)
    dec_wkv = draw_dec_wkv(jax.random.fold_in(arg_keys[20], 71), 0)
    dec_bv = normal_values(arg_keys[12], (KVG, HD), 0.5, 3.0, (), jnp.float32)
    text = normal_values(arg_keys[13], (ROWS, D), 1.0, 6.0, ((0, 8),))
    norm_gain = jnp.clip(1.0 + 0.15 * jax.random.normal(arg_keys[14], (D,), jnp.float32), 0.25, 1.75)
    dec_wq = normal_values(arg_keys[15], (D, KVG * QPG * HD), D ** -0.5, 0.0625, ((0, 8), (1, 4)))
    dec_bq = normal_values(arg_keys[16], (KVG * QPG * HD,), 0.5, 3.0, ((0, 4),), jnp.float32)
    dec_wo = heavy_noise(arg_keys[17], (KVG * QPG * HD, D), (KVG * QPG * HD) ** -0.5, 0.125, ((0, 4), (1, 8)), (0, 1, 8, 2.0))
    span_start = draw_span_start(jax.random.fold_in(arg_keys[20], 71), 0)
    span_len = draw_span_len(jax.random.fold_in(arg_keys[20], 71), 0)
    return dict(audio=audio, ln_gain=ln_gain, ln_shift=ln_shift, enc_wq=enc_wq, enc_bq=enc_bq, enc_wk=enc_wk, enc_wv=enc_wv, enc_bv=enc_bv, enc_wo=enc_wo, enc_bo=enc_bo, windows=windows, dec_wkv=dec_wkv, dec_bv=dec_bv, text=text, norm_gain=norm_gain, dec_wq=dec_wq, dec_bq=dec_bq, dec_wo=dec_wo, span_start=span_start, span_len=span_len)


def layer_norm(values, gain, shift):
    values = values.astype(jnp.float32)
    centre = values - lax.optimization_barrier(jnp.mean(values, axis=-1, keepdims=True))
    spread = lax.optimization_barrier(jnp.mean(centre * centre, axis=-1, keepdims=True))
    return centre * lax.rsqrt(spread + 1e-05) * gain + shift

def rms_norm(values, gain):
    values = values.astype(jnp.float32)
    return values * lax.rsqrt(lax.optimization_barrier(jnp.mean(values * values, axis=-1, keepdims=True)) + 1e-06) * gain

def masked_softmax(scores, valid):
    highest = lax.optimization_barrier(jnp.max(jnp.where(valid, scores, -jnp.inf), axis=-1, keepdims=True))
    raised = jnp.where(valid, jnp.exp(scores - highest), jnp.zeros_like(scores))
    return (raised / lax.optimization_barrier(jnp.sum(raised, axis=-1, keepdims=True))).astype(jnp.bfloat16)

def reference(audio, ln_gain, ln_shift, enc_wq, enc_bq, enc_wk, enc_wv, enc_bv, enc_wo, enc_bo, windows, dec_wkv, dec_bv, text, norm_gain, dec_wq, dec_bq, dec_wo, span_start, span_len):
    hidden = layer_norm(audio, ln_gain, ln_shift).astype(jnp.bfloat16)
    enc_query = (jnp.dot(hidden, enc_wq, preferred_element_type=jnp.float32) + enc_bq).astype(jnp.bfloat16)
    enc_keys = jnp.dot(hidden, enc_wk, preferred_element_type=jnp.float32).astype(jnp.bfloat16)
    enc_values = (jnp.dot(hidden, enc_wv, preferred_element_type=jnp.float32) + enc_bv).astype(jnp.bfloat16)
    enc_query = enc_query.reshape(FRAMES, EH, EHD)
    pad_keys = jnp.pad(enc_keys.reshape(FRAMES, EH, EHD), ((EWIN, EWIN), (0, 0), (0, 0)))
    pad_values = jnp.pad(enc_values.reshape(FRAMES, EH, EHD), ((EWIN, EWIN), (0, 0), (0, 0)))
    extent = FR_SEQ + 2 * EWIN

    def enc_block(block_index):
        first_frame = block_index * FR_SEQ
        query_block = lax.dynamic_slice_in_dim(enc_query, first_frame, FR_SEQ, 0).astype(jnp.float32)
        key_block = lax.dynamic_slice_in_dim(pad_keys, first_frame, extent, 0).astype(jnp.float32)
        value_block = lax.dynamic_slice_in_dim(pad_values, first_frame, extent, 0).astype(jnp.float32)
        scores = jnp.einsum('qhd,khd->hqk', query_block, key_block) * EHD ** (-0.5)
        row_frames = first_frame + jnp.arange(FR_SEQ, dtype=jnp.int32)
        col_frames = first_frame - EWIN + jnp.arange(extent, dtype=jnp.int32)
        distance = jnp.abs(row_frames[:, None] - col_frames[None, :])
        inside = (col_frames >= 0) & (col_frames < FRAMES)
        valid = (distance[None, :, :] <= windows[:, None, None]) & inside[None, None, :]
        weights = masked_softmax(scores, valid)
        context = jnp.einsum('hqk,khd->qhd', weights.astype(jnp.float32), value_block)
        return context.astype(jnp.bfloat16)
    enc_context = lax.map(enc_block, jnp.arange(N_SEQ, dtype=jnp.int32)).reshape(FRAMES, EH * EHD)
    mixed = jnp.dot(enc_context, enc_wo, preferred_element_type=jnp.float32)
    enc_out = (audio.astype(jnp.float32) + mixed + enc_bo).astype(jnp.bfloat16)
    band_bias = jnp.concatenate([jnp.zeros_like(dec_bv), dec_bv], axis=1)
    band_kv = jnp.dot(enc_out, dec_wkv.reshape(D_ENC, KVG * 2 * HD), preferred_element_type=jnp.float32)
    band_kv = (band_kv.reshape(FRAMES, KVG, 2 * HD) + band_bias).astype(jnp.bfloat16)
    pad_band = jnp.pad(band_kv, ((BAND, BAND), (0, 0), (0, 0)))
    normed = rms_norm(text, norm_gain).astype(jnp.bfloat16)
    dec_query = (jnp.dot(normed, dec_wq, preferred_element_type=jnp.float32) + dec_bq).astype(jnp.bfloat16)
    dec_query = dec_query.reshape(ROWS, KVG, QPG, HD)
    band_extent = FR_SEQ + 2 * BAND
    set_width = GL * QPG * HD

    def dec_block(block_index):
        first_row = block_index * ROWS_DEV
        first_frame = block_index * FR_SEQ
        query_block = lax.dynamic_slice_in_dim(dec_query, first_row, ROWS_DEV, 0).astype(jnp.float32)
        pair_block = lax.dynamic_slice_in_dim(pad_band, first_frame, band_extent, 0).astype(jnp.float32)
        key_block = pair_block[:, :, :HD]
        value_block = pair_block[:, :, HD:]
        scores = jnp.einsum('rgqd,kgd->rgqk', query_block, key_block) * HD ** (-0.5)
        begins = lax.dynamic_slice_in_dim(span_start, first_row, ROWS_DEV, 0)
        counts = lax.dynamic_slice_in_dim(span_len, first_row, ROWS_DEV, 0)
        col_frames = first_frame - BAND + jnp.arange(band_extent, dtype=jnp.int32)
        valid = (col_frames[None, :] >= begins[:, None]) & (col_frames[None, :] < (begins + counts)[:, None])
        weights = masked_softmax(scores, valid[:, None, None, :])
        context = jnp.einsum('rgqk,kgd->rgqd', weights.astype(jnp.float32), value_block)
        context = context.astype(jnp.bfloat16).reshape(ROWS_DEV, KVG * QPG * HD)
        total = jnp.zeros((ROWS_DEV, D), jnp.float32)
        for head_set in range(N_HEADS):
            term = jnp.dot(context[:, head_set * set_width:(head_set + 1) * set_width], dec_wo[head_set * set_width:(head_set + 1) * set_width], preferred_element_type=jnp.float32)
            total = total + lax.optimization_barrier(term.astype(jnp.bfloat16)).astype(jnp.float32)
        text_block = lax.dynamic_slice_in_dim(text, first_row, ROWS_DEV, 0)
        return (text_block.astype(jnp.float32) + total).astype(jnp.bfloat16)
    dec_out = lax.map(dec_block, jnp.arange(N_SEQ, dtype=jnp.int32)).reshape(ROWS, D)
    return (enc_out, dec_out)
```

```python
import functools

import jax
import jax.numpy as jnp
from jax import lax
from jax.experimental import pallas as pl
from jax.experimental.pallas import tpu as pltpu
from jax.sharding import PartitionSpec as P

EWIN = 128
BAND = 256


def with_halo(block, sides, width):
    for axis, dim in sides:
        count = lax.axis_size(axis)
        forward = [(i, i + 1) for i in range(count - 1)]
        backward = [(target, source) for source, target in forward]
        low = lax.ppermute(
            lax.slice_in_dim(block, block.shape[dim] - width, None, axis=dim), axis, forward
        )
        high = lax.ppermute(lax.slice_in_dim(block, 0, width, axis=dim), axis, backward)
        block = jnp.concatenate([low, block, high], axis=dim)
    return block


def shifted(count, offset):
    return [(i, (i + offset) % count) for i in range(count)]


MESH = pl.DeviceIdType.MESH
TILE = 256


def query_kernel(
    depth_z,
    depth_x,
    heads,
    own_ref,
    weight_ref,
    bias_ref,
    out_ref,
    rows_all,
    turned,
    turned_in,
    summed,
    summed_in,
    total,
    local_sem,
    spread_send,
    rows_recv,
    share_send,
    turn_send,
    turn_recv,
    sum_send,
    sum_recv,
):
    seq = depth_z * depth_x
    me = lax.axis_index("seq")
    head = lax.axis_index("heads")
    my_z, my_x = me // depth_x, lax.rem(me, depth_x)
    width = weight_ref.shape[1]
    tile = min(TILE, width)
    rows = rows_all.shape[1] * rows_all.shape[2]

    barrier = pltpu.get_barrier_semaphore()
    for step in range(1, seq):
        pl.semaphore_signal(
            barrier, inc=1, device_id=(lax.rem(me + step, seq), head), device_id_type=MESH
        )
    for step in range(1, heads):
        pl.semaphore_signal(
            barrier, inc=1, device_id=(me, lax.rem(head + step, heads)), device_id_type=MESH
        )
    pl.semaphore_wait(barrier, seq - 1 + heads - 1)

    started = []

    def send(source, target, send_sem, recv_sem, device):
        copy = pltpu.make_async_remote_copy(
            src_ref=source,
            dst_ref=target,
            send_sem=send_sem,
            recv_sem=recv_sem,
            device_id=device,
            device_id_type=MESH,
        )
        copy.start()
        started.append(copy)

    def arrived(target, recv_sem):
        pltpu.make_async_copy(target, target, recv_sem).wait()

    for step in range(1, seq):
        goal = lax.rem(me + step, seq)
        send(
            own_ref.at[goal],
            rows_all.at[me, head],
            spread_send.at[step - 1],
            rows_recv.at[me, head],
            (goal, head),
        )
    own_copy = pltpu.make_async_copy(own_ref.at[me], rows_all.at[me, head], local_sem)
    own_copy.start()
    own_copy.wait()
    for step in range(seq):
        source = lax.rem(me + seq - step, seq)
        if step:
            arrived(rows_all.at[source, head], rows_recv.at[source, head])
        for turn in range(1, heads):
            send(
                rows_all.at[source, head],
                rows_all.at[source, head],
                share_send.at[step, turn - 1],
                rows_recv.at[source, head],
                (me, lax.rem(head + turn, heads)),
            )

    def complete(block):
        for turn in range(1, heads):
            other = lax.rem(head + turn, heads)
            arrived(rows_all.at[block, other], rows_recv.at[block, other])

    def multiply(block, store):
        values = rows_all.at[block]

        def body(index, carry):
            columns = pl.ds(pl.multiple_of(index * tile, tile), tile)
            product = jnp.dot(
                values[...].reshape(rows, values.shape[2]),
                weight_ref[:, columns],
                preferred_element_type=jnp.float32,
            )
            store(columns, product)
            return carry

        lax.fori_loop(0, width // tile, body, 0)

    for i in range(depth_z):
        goal_z = lax.rem(my_z + depth_z - i, depth_z)
        for j in range(1, depth_x):
            goal_x = lax.rem(my_x + depth_x - j, depth_x)
            block = goal_z * depth_x + goal_x
            complete(block)

            def keep(columns, product, i=i, j=j):
                turned[j - 1, i, :, columns] = product.astype(jnp.bfloat16)

            multiply(block, keep)
            send(
                turned.at[j - 1, i],
                turned_in.at[j - 1, i],
                turn_send.at[j - 1, i],
                turn_recv.at[j - 1, i],
                (my_z * depth_x + goal_x, head),
            )

    for i in [*range(1, depth_z), 0]:
        goal_z = lax.rem(my_z + depth_z - i, depth_z)
        block = goal_z * depth_x + my_x
        complete(block)
        for j in range(1, depth_x):
            arrived(turned_in.at[j - 1, i], turn_recv.at[j - 1, i])

        def add(columns, product, i=i):
            for j in range(1, depth_x):
                product += turned_in[j - 1, i, :, columns].astype(jnp.float32)
            if i:
                summed[i - 1, :, columns] = product.astype(jnp.bfloat16)
            else:
                total[:, columns] = product

        multiply(block, add)
        if i:
            send(
                summed.at[i - 1],
                summed_in.at[i - 1],
                sum_send.at[i - 1],
                sum_recv.at[i - 1],
                (goal_z * depth_x + my_x, head),
            )

    for i in range(1, depth_z):
        arrived(summed_in.at[i - 1], sum_recv.at[i - 1])

    def finish(index, carry):
        columns = pl.ds(pl.multiple_of(index * tile, tile), tile)
        result = total[:, columns] + bias_ref[:, columns]
        for i in range(1, depth_z):
            result += summed_in[i - 1, :, columns].astype(jnp.float32)
        out_ref[:, columns] = result.astype(jnp.bfloat16)
        return carry

    lax.fori_loop(0, width // tile, finish, 0)
    for copy in started:
        copy.wait_send()


def project_queries(own_rows, weight, bias):
    seq = lax.axis_size("seq")
    heads = lax.axis_size("heads")
    depth_z = 4 if seq % 4 == 0 else seq
    depth_x = seq // depth_z
    quarter = own_rows.shape[1]
    depth, width = weight.shape
    rows = quarter * heads
    turns = max(depth_x - 1, 1)
    sums = max(depth_z - 1, 1)
    vmem = pl.BlockSpec(memory_space=pltpu.VMEM)
    dma = pltpu.SemaphoreType.DMA
    return pl.pallas_call(
        functools.partial(query_kernel, depth_z, depth_x, heads),
        out_shape=jax.ShapeDtypeStruct((rows, width), jnp.bfloat16),
        in_specs=[vmem] * 3,
        out_specs=vmem,
        scratch_shapes=[
            pltpu.VMEM((seq, heads, quarter, depth), jnp.bfloat16),
            pltpu.VMEM((turns, depth_z, rows, width), jnp.bfloat16),
            pltpu.VMEM((turns, depth_z, rows, width), jnp.bfloat16),
            pltpu.VMEM((sums, rows, width), jnp.bfloat16),
            pltpu.VMEM((sums, rows, width), jnp.bfloat16),
            pltpu.VMEM((rows, width), jnp.float32),
            dma,
            dma((seq,)),
            dma((seq, heads)),
            dma((seq, heads)),
            dma((turns, depth_z)),
            dma((turns, depth_z)),
            dma((sums,)),
            dma((sums,)),
        ],
        compiler_params=pltpu.CompilerParams(
            collective_id=0, has_side_effects=True, vmem_limit_bytes=48 * 2**20
        ),
        cost_estimate=pl.CostEstimate(
            flops=2 * rows * seq * depth * width,
            bytes_accessed=400 * 2**20,
            transcendentals=0,
        ),
    )(own_rows, weight, bias.reshape(1, width))


def output_kernel(
    depth_z,
    depth_x,
    heads,
    own_ref,
    weight_ref,
    out_ref,
    rows_all,
    terms,
    terms_in,
    summed,
    final_in,
    local_sem,
    line_send,
    turn_send,
    rows_recv,
    term_send,
    term_recv,
    final_send,
    final_recv,
):
    seq = depth_z * depth_x
    group = seq // heads
    me = lax.axis_index("seq")
    head = lax.axis_index("heads")
    my_z, my_x = me // depth_x, lax.rem(me, depth_x)
    owner, slot = me // group, lax.rem(me, group)
    width = weight_ref.shape[1]
    tile = min(TILE, width)
    quarter = summed.shape[1]

    barrier = pltpu.get_barrier_semaphore()
    for step in range(1, depth_z):
        goal = lax.rem(my_z + step, depth_z) * depth_x + my_x
        pl.semaphore_signal(barrier, inc=1, device_id=(goal, head), device_id_type=MESH)
    for step in range(1, depth_x):
        goal = my_z * depth_x + lax.rem(my_x + step, depth_x)
        pl.semaphore_signal(barrier, inc=1, device_id=(goal, head), device_id_type=MESH)
    for step in range(1, heads):
        pl.semaphore_signal(
            barrier, inc=1, device_id=(me, lax.rem(head + step, heads)), device_id_type=MESH
        )
    for part in range(group):
        for other in range(heads):
            source = head * group + part

            @pl.when(jnp.logical_or(source != me, head != other))
            def _():
                pl.semaphore_signal(
                    barrier, inc=1, device_id=(source, other), device_id_type=MESH
                )

    self_target = jnp.where(owner == head, 1, 0)
    pl.semaphore_wait(
        barrier, depth_z - 1 + depth_x - 1 + heads - 1 + seq - self_target
    )

    started = []

    def send(source, target, send_sem, recv_sem, device):
        copy = pltpu.make_async_remote_copy(
            src_ref=source,
            dst_ref=target,
            send_sem=send_sem,
            recv_sem=recv_sem,
            device_id=device,
            device_id_type=MESH,
        )
        copy.start()
        started.append(copy)

    def arrived(target, recv_sem):
        pltpu.make_async_copy(target, target, recv_sem).wait()

    for step in range(1, depth_z):
        goal = lax.rem(my_z + step, depth_z) * depth_x + my_x
        send(own_ref, rows_all.at[me], line_send.at[step - 1], rows_recv.at[me], (goal, head))
    own_copy = pltpu.make_async_copy(own_ref, rows_all.at[me], local_sem)
    own_copy.start()
    own_copy.wait()

    def work(block, place):
        def body(index, carry):
            columns = pl.ds(pl.multiple_of(index * tile, tile), tile)
            terms[block, :, columns] = jnp.dot(
                rows_all[block], weight_ref[:, columns], preferred_element_type=jnp.float32
            ).astype(jnp.bfloat16)
            return carry

        lax.fori_loop(0, width // tile, body, 0)
        for turn in range(1, heads):
            other = lax.rem(head + turn, heads)
            start = pl.multiple_of(other * quarter, quarter)
            send(
                terms.at[block, pl.ds(start, quarter)],
                terms_in.at[turn - 1, block],
                term_send.at[place, turn - 1],
                term_recv.at[turn - 1, block],
                (me, other),
            )

    def finish(block):
        start = pl.multiple_of(head * quarter, quarter)
        result = terms[block, pl.ds(start, quarter)].astype(jnp.float32)
        for turn in range(1, heads):
            arrived(terms_in.at[turn - 1, block], term_recv.at[turn - 1, block])
            result += terms_in[turn - 1, block].astype(jnp.float32)
        summed[block] = result.astype(jnp.bfloat16)
        local = jnp.logical_and(block == me, owner == head)

        @pl.when(local)
        def _():
            final_in[slot, head] = summed[block]

        @pl.when(jnp.logical_not(local))
        def _():
            pltpu.make_async_remote_copy(
                src_ref=summed.at[block],
                dst_ref=final_in.at[slot, head],
                send_sem=final_send.at[block],
                recv_sem=final_recv.at[slot, head],
                device_id=(block, owner),
                device_id_type=MESH,
            ).start()

    order = [(i, j) for i in range(depth_z) for j in range(depth_x)]

    def block_of(i, j):
        return lax.rem(my_z + depth_z - i, depth_z) * depth_x + lax.rem(
            my_x + depth_x - j, depth_x
        )

    lag = 2 * depth_x
    for place, (i, j) in enumerate(order):
        block = block_of(i, j)
        if j == 0:
            if i:
                arrived(rows_all.at[block], rows_recv.at[block])
            for step in range(1, depth_x):
                goal = my_z * depth_x + lax.rem(my_x + step, depth_x)
                send(
                    rows_all.at[block],
                    rows_all.at[block],
                    turn_send.at[i, step - 1],
                    rows_recv.at[block],
                    (goal, head),
                )
        else:
            arrived(rows_all.at[block], rows_recv.at[block])
        work(block, place)
        if place >= lag:
            finish(block_of(*order[place - lag]))
    for pair in order[-lag:]:
        finish(block_of(*pair))
    for part in range(group):
        for other in range(heads):
            source = head * group + part

            @pl.when(jnp.logical_or(source != me, head != other))
            def _():
                arrived(final_in.at[part, other], final_recv.at[part, other])

            out_ref[pl.ds(other * quarter, quarter), pl.ds(part * width, width)] = final_in[
                part, other
            ]
    for copy in started:
        copy.wait_send()
    for block in range(seq):

        @pl.when(jnp.logical_not(jnp.logical_and(block == me, owner == head)))
        def _():
            arrived(summed.at[block], final_send.at[block])


def project_outputs(rows_own, weight):
    seq = lax.axis_size("seq")
    heads = lax.axis_size("heads")
    depth_z = 4 if seq % 4 == 0 else seq
    depth_x = seq // depth_z
    group = seq // heads
    rows, depth = rows_own.shape
    width = weight.shape[1]
    quarter = rows // heads
    turns = max(depth_x - 1, 1)
    vmem = pl.BlockSpec(memory_space=pltpu.VMEM)
    dma = pltpu.SemaphoreType.DMA
    return pl.pallas_call(
        functools.partial(output_kernel, depth_z, depth_x, heads),
        out_shape=jax.ShapeDtypeStruct((rows, group * width), jnp.bfloat16),
        in_specs=[vmem] * 2,
        out_specs=vmem,
        scratch_shapes=[
            pltpu.VMEM((seq, rows, depth), jnp.bfloat16),
            pltpu.VMEM((seq, rows, width), jnp.bfloat16),
            pltpu.VMEM((heads - 1, seq, quarter, width), jnp.bfloat16),
            pltpu.VMEM((seq, quarter, width), jnp.bfloat16),
            pltpu.VMEM((group, heads, quarter, width), jnp.bfloat16),
            dma,
            dma((depth_z,)),
            dma((depth_z, turns)),
            dma((seq,)),
            dma((seq, heads - 1)),
            dma((heads - 1, seq)),
            dma((seq,)),
            dma((group, heads)),
        ],
        compiler_params=pltpu.CompilerParams(
            collective_id=1, has_side_effects=True, vmem_limit_bytes=48 * 2**20
        ),
        cost_estimate=pl.CostEstimate(
            flops=2 * rows * seq * depth * width,
            bytes_accessed=400 * 2**20,
            transcendentals=0,
        ),
    )(rows_own, weight)


def layer_norm(values, gain, shift):
    values = values.astype(jnp.float32)
    centre = values - jnp.mean(values, axis=-1, keepdims=True)
    spread = jnp.mean(centre * centre, axis=-1, keepdims=True)
    return centre * lax.rsqrt(spread + 1e-05) * gain + shift


def rms_norm(values, gain):
    values = values.astype(jnp.float32)
    return values * lax.rsqrt(jnp.mean(values * values, axis=-1, keepdims=True) + 1e-06) * gain


def masked_softmax(scores, valid):
    highest = jnp.max(jnp.where(valid, scores, -jnp.inf), axis=-1, keepdims=True)
    raised = jnp.where(valid, jnp.exp(scores - highest), jnp.zeros_like(scores))
    return (raised / jnp.sum(raised, axis=-1, keepdims=True)).astype(jnp.bfloat16)


def shards(
    audio,
    ln_gain,
    ln_shift,
    enc_wq,
    enc_bq,
    enc_wk,
    enc_wv,
    enc_bv,
    enc_wo,
    enc_bo,
    windows,
    dec_wkv,
    dec_bv,
    text,
    norm_gain,
    dec_wq,
    dec_bq,
    dec_wo,
    span_start,
    span_len,
):
    seq_count = lax.axis_size("seq")
    head_count = lax.axis_size("heads")
    seq_index = lax.axis_index("seq")
    head_index = lax.axis_index("heads")
    frames_dev = audio.shape[0]
    enc_width = audio.shape[1]
    heads_dev = windows.shape[0]
    head_size = enc_wq.shape[1] // heads_dev
    all_frames = frames_dev * seq_count
    hidden = layer_norm(audio, ln_gain, ln_shift).astype(jnp.bfloat16)
    enc_query = (jnp.dot(hidden, enc_wq, preferred_element_type=jnp.float32) + enc_bq).astype(
        jnp.bfloat16
    )
    enc_keys = jnp.dot(hidden, enc_wk, preferred_element_type=jnp.float32).astype(jnp.bfloat16)
    enc_values = (jnp.dot(hidden, enc_wv, preferred_element_type=jnp.float32) + enc_bv).astype(
        jnp.bfloat16
    )
    enc_pairs = jnp.stack([enc_keys, enc_values], axis=1)
    widened = with_halo(enc_pairs, (("seq", 0),), EWIN)
    extent = frames_dev + 2 * EWIN
    key_block = widened[:, 0, :].reshape(extent, heads_dev, head_size)
    value_block = widened[:, 1, :].reshape(extent, heads_dev, head_size)
    query_block = enc_query.reshape(frames_dev, heads_dev, head_size)
    scores = jnp.einsum(
        "qhd,khd->hqk", query_block, key_block, preferred_element_type=jnp.float32
    ) * head_size ** (-0.5)
    row_frames = seq_index * frames_dev + jnp.arange(frames_dev, dtype=jnp.int32)
    col_frames = seq_index * frames_dev - EWIN + jnp.arange(extent, dtype=jnp.int32)
    distance = jnp.abs(row_frames[:, None] - col_frames[None, :])
    inside = (col_frames >= 0) & (col_frames < all_frames)
    valid = (distance[None, :, :] <= windows[:, None, None]) & inside[None, None, :]
    enc_weights = masked_softmax(scores, valid)
    enc_context = jnp.einsum(
        "hqk,khd->qhd", enc_weights, value_block, preferred_element_type=jnp.float32
    )
    enc_context = enc_context.astype(jnp.bfloat16).reshape(frames_dev, heads_dev * head_size)
    enc_term = jnp.dot(enc_context, enc_wo, preferred_element_type=jnp.float32)
    share = frames_dev // head_count
    pieces = enc_term.astype(jnp.bfloat16).reshape(head_count, share, enc_width)
    mixed = lax.dynamic_index_in_dim(pieces, head_index, 0, False).astype(jnp.float32)
    for turn in range(1, head_count):
        piece = lax.dynamic_index_in_dim(pieces, (head_index + turn) % head_count, 0, False)
        mixed += lax.ppermute(piece, "heads", shifted(head_count, turn)).astype(jnp.float32)
    own_audio = lax.dynamic_slice_in_dim(audio, head_index * share, share, 0)
    enc_out = (own_audio.astype(jnp.float32) + mixed + enc_bo).astype(jnp.bfloat16)
    groups_dev = dec_wkv.shape[1] // head_count
    pair_width = dec_wkv.shape[2]
    dec_head = pair_width // 2
    band_bias = jnp.concatenate([jnp.zeros_like(dec_bv), dec_bv], axis=1)
    frames_all = jnp.zeros((head_count, share, enc_width), jnp.bfloat16)
    frames_all = lax.dynamic_update_index_in_dim(frames_all, enc_out, head_index, 0)
    for turn in range(1, head_count):
        frames_all = lax.dynamic_update_index_in_dim(
            frames_all,
            lax.ppermute(enc_out, "heads", shifted(head_count, turn)),
            (head_index + head_count - turn) % head_count,
            0,
        )
    frames_all = frames_all.reshape(frames_dev, enc_width)
    weight_group = lax.dynamic_slice_in_dim(
        dec_wkv, head_index * groups_dev, groups_dev, 1
    ).reshape(enc_width, groups_dev * pair_width)
    bias_group = lax.dynamic_slice_in_dim(
        band_bias, head_index * groups_dev, groups_dev, 0
    ).reshape(groups_dev * pair_width)
    band_pairs = (
        jnp.dot(frames_all, weight_group, preferred_element_type=jnp.float32) + bias_group
    ).astype(jnp.bfloat16)
    band_pairs = band_pairs.reshape(frames_dev, groups_dev, pair_width)
    band_wide = with_halo(band_pairs, (("seq", 0),), BAND)
    rows_dev = text.shape[0]
    model_width = text.shape[1]
    query_width = dec_wq.shape[1]
    query_heads = query_width // (groups_dev * dec_head)
    quarter = rows_dev // head_count
    depth = dec_wq.shape[0]
    own_rows = lax.dynamic_slice_in_dim(text, head_index * quarter, quarter, 0)
    normed = rms_norm(own_rows, norm_gain).astype(jnp.bfloat16)
    normed = normed.reshape(quarter, seq_count, depth).transpose(1, 0, 2)
    dec_query = project_queries(normed, dec_wq, dec_bq).reshape(
        rows_dev, groups_dev, query_heads, dec_head
    )
    band_extent = band_wide.shape[0]
    band_keys = band_wide[:, :, :dec_head]
    band_values = band_wide[:, :, dec_head:]
    dec_scores = jnp.einsum(
        "rgqd,kgd->rgqk", dec_query, band_keys, preferred_element_type=jnp.float32
    ) * dec_head ** (-0.5)
    band_frames = seq_index * frames_dev - BAND + jnp.arange(band_extent, dtype=jnp.int32)
    in_band = (band_frames[None, :] >= span_start[:, None]) & (
        band_frames[None, :] < (span_start + span_len)[:, None]
    )
    dec_weights = masked_softmax(dec_scores, in_band[:, None, None, :])
    dec_context = jnp.einsum(
        "rgqk,kgd->rgqd", dec_weights, band_values, preferred_element_type=jnp.float32
    )
    dec_context = dec_context.astype(jnp.bfloat16).reshape(rows_dev, query_width)
    summed = project_outputs(dec_context, dec_wo).astype(jnp.float32)
    col_share = model_width // head_count
    own_text = lax.dynamic_slice_in_dim(text, head_index * col_share, col_share, 1)
    dec_out = (own_text.astype(jnp.float32) + summed).astype(jnp.bfloat16)
    return (enc_out, dec_out)


def solution(mesh):
    return jax.shard_map(
        shards,
        mesh=mesh,
        in_specs=(
            P("seq", None),
            P(),
            P(),
            P(None, "heads"),
            P("heads"),
            P(None, "heads"),
            P(None, "heads"),
            P("heads"),
            P("heads", None),
            P(),
            P("heads"),
            P(),
            P(),
            P("seq", None),
            P(),
            P("seq", "heads"),
            P("heads"),
            P("heads", "seq"),
            P("seq"),
            P("seq"),
        ),
        out_specs=(P(("seq", "heads"), None), P("seq", "heads")),
        check_vma=False,
    )
```

```python
import functools

import jax
import jax.numpy as jnp
from jax import lax
from jax.experimental import pallas as pl
from jax.experimental.pallas import tpu as pltpu
from jax.sharding import PartitionSpec as P

EWIN = 128
BAND = 256


def with_halo(block, sides, width):
    for axis, dim in sides:
        count = lax.axis_size(axis)
        forward = [(i, i + 1) for i in range(count - 1)]
        backward = [(target, source) for source, target in forward]
        low = lax.ppermute(
            lax.slice_in_dim(block, block.shape[dim] - width, None, axis=dim), axis, forward
        )
        high = lax.ppermute(lax.slice_in_dim(block, 0, width, axis=dim), axis, backward)
        block = jnp.concatenate([low, block, high], axis=dim)
    return block


def shifted(count, offset):
    return [(i, (i + offset) % count) for i in range(count)]


MESH = pl.DeviceIdType.MESH
TILE = 256


def query_kernel(
    depth_z,
    depth_x,
    heads,
    own_ref,
    weight_ref,
    bias_ref,
    out_ref,
    rows_all,
    turned,
    turned_in,
    summed,
    summed_in,
    total,
    local_sem,
    spread_send,
    rows_recv,
    share_send,
    turn_send,
    turn_recv,
    sum_send,
    sum_recv,
):
    seq = depth_z * depth_x
    me = lax.axis_index("seq")
    head = lax.axis_index("heads")
    my_z, my_x = me // depth_x, lax.rem(me, depth_x)
    width = weight_ref.shape[1]
    tile = min(TILE, width)
    rows = rows_all.shape[1] * rows_all.shape[2]

    barrier = pltpu.get_barrier_semaphore()
    for step in range(1, seq):
        pl.semaphore_signal(
            barrier, inc=1, device_id=(lax.rem(me + step, seq), head), device_id_type=MESH
        )
    for step in range(1, heads):
        pl.semaphore_signal(
            barrier, inc=1, device_id=(me, lax.rem(head + step, heads)), device_id_type=MESH
        )
    pl.semaphore_wait(barrier, seq - 1 + heads - 1)

    started = []

    def send(source, target, send_sem, recv_sem, device):
        copy = pltpu.make_async_remote_copy(
            src_ref=source,
            dst_ref=target,
            send_sem=send_sem,
            recv_sem=recv_sem,
            device_id=device,
            device_id_type=MESH,
        )
        copy.start()
        started.append(copy)

    def arrived(target, recv_sem):
        pltpu.make_async_copy(target, target, recv_sem).wait()

    for step in range(1, seq):
        goal = lax.rem(me + step, seq)
        send(
            own_ref.at[goal],
            rows_all.at[me, head],
            spread_send.at[step - 1],
            rows_recv.at[me, head],
            (goal, head),
        )
    own_copy = pltpu.make_async_copy(own_ref.at[me], rows_all.at[me, head], local_sem)
    own_copy.start()
    own_copy.wait()
    for step in range(seq):
        source = lax.rem(me + seq - step, seq)
        if step:
            arrived(rows_all.at[source, head], rows_recv.at[source, head])
        for turn in range(1, heads):
            send(
                rows_all.at[source, head],
                rows_all.at[source, head],
                share_send.at[step, turn - 1],
                rows_recv.at[source, head],
                (me, lax.rem(head + turn, heads)),
            )

    def complete(block):
        for turn in range(1, heads):
            other = lax.rem(head + turn, heads)
            arrived(rows_all.at[block, other], rows_recv.at[block, other])

    def multiply(block, store):
        values = rows_all.at[block]

        def body(index, carry):
            columns = pl.ds(pl.multiple_of(index * tile, tile), tile)
            product = jnp.dot(
                values[...].reshape(rows, values.shape[2]),
                weight_ref[:, columns],
                preferred_element_type=jnp.float32,
            )
            store(columns, product)
            return carry

        lax.fori_loop(0, width // tile, body, 0)

    for i in range(depth_z):
        goal_z = lax.rem(my_z + depth_z - i, depth_z)
        for j in range(1, depth_x):
            goal_x = lax.rem(my_x + depth_x - j, depth_x)
            block = goal_z * depth_x + goal_x
            complete(block)

            def keep(columns, product, i=i, j=j):
                turned[j - 1, i, :, columns] = product.astype(jnp.bfloat16)

            multiply(block, keep)
            send(
                turned.at[j - 1, i],
                turned_in.at[j - 1, i],
                turn_send.at[j - 1, i],
                turn_recv.at[j - 1, i],
                (my_z * depth_x + goal_x, head),
            )

    for i in [*range(1, depth_z), 0]:
        goal_z = lax.rem(my_z + depth_z - i, depth_z)
        block = goal_z * depth_x + my_x
        complete(block)
        for j in range(1, depth_x):
            arrived(turned_in.at[j - 1, i], turn_recv.at[j - 1, i])

        def add(columns, product, i=i):
            for j in range(1, depth_x):
                product += turned_in[j - 1, i, :, columns].astype(jnp.float32)
            if i:
                summed[i - 1, :, columns] = product.astype(jnp.bfloat16)
            else:
                total[:, columns] = product

        multiply(block, add)
        if i:
            send(
                summed.at[i - 1],
                summed_in.at[i - 1],
                sum_send.at[i - 1],
                sum_recv.at[i - 1],
                (goal_z * depth_x + my_x, head),
            )

    for i in range(1, depth_z):
        arrived(summed_in.at[i - 1], sum_recv.at[i - 1])

    def finish(index, carry):
        columns = pl.ds(pl.multiple_of(index * tile, tile), tile)
        result = total[:, columns] + bias_ref[:, columns]
        for i in range(1, depth_z):
            result += summed_in[i - 1, :, columns].astype(jnp.float32)
        out_ref[:, columns] = result.astype(jnp.bfloat16)
        return carry

    lax.fori_loop(0, width // tile, finish, 0)
    for copy in started:
        copy.wait_send()


def project_queries(own_rows, weight, bias):
    seq = lax.axis_size("seq")
    heads = lax.axis_size("heads")
    depth_z = 4 if seq % 4 == 0 else seq
    depth_x = seq // depth_z
    quarter = own_rows.shape[1]
    depth, width = weight.shape
    rows = quarter * heads
    turns = max(depth_x - 1, 1)
    sums = max(depth_z - 1, 1)
    vmem = pl.BlockSpec(memory_space=pltpu.VMEM)
    dma = pltpu.SemaphoreType.DMA
    return pl.pallas_call(
        functools.partial(query_kernel, depth_z, depth_x, heads),
        out_shape=jax.ShapeDtypeStruct((rows, width), jnp.bfloat16),
        in_specs=[vmem] * 3,
        out_specs=vmem,
        scratch_shapes=[
            pltpu.VMEM((seq, heads, quarter, depth), jnp.bfloat16),
            pltpu.VMEM((turns, depth_z, rows, width), jnp.bfloat16),
            pltpu.VMEM((turns, depth_z, rows, width), jnp.bfloat16),
            pltpu.VMEM((sums, rows, width), jnp.bfloat16),
            pltpu.VMEM((sums, rows, width), jnp.bfloat16),
            pltpu.VMEM((rows, width), jnp.float32),
            dma,
            dma((seq,)),
            dma((seq, heads)),
            dma((seq, heads)),
            dma((turns, depth_z)),
            dma((turns, depth_z)),
            dma((sums,)),
            dma((sums,)),
        ],
        compiler_params=pltpu.CompilerParams(
            collective_id=0, has_side_effects=True, vmem_limit_bytes=48 * 2**20
        ),
        cost_estimate=pl.CostEstimate(
            flops=2 * rows * seq * depth * width,
            bytes_accessed=400 * 2**20,
            transcendentals=0,
        ),
    )(own_rows, weight, bias.reshape(1, width))


def output_kernel(
    depth_z,
    depth_x,
    heads,
    own_ref,
    weight_ref,
    out_ref,
    rows_all,
    terms,
    terms_in,
    summed,
    final_in,
    local_sem,
    line_send,
    turn_send,
    rows_recv,
    term_send,
    term_recv,
    final_send,
    final_recv,
):
    seq = depth_z * depth_x
    group = seq // heads
    me = lax.axis_index("seq")
    head = lax.axis_index("heads")
    my_z, my_x = me // depth_x, lax.rem(me, depth_x)
    owner, slot = me // group, lax.rem(me, group)
    width = weight_ref.shape[1]
    tile = min(TILE, width)
    quarter = summed.shape[1]

    barrier = pltpu.get_barrier_semaphore()
    for step in range(1, depth_z):
        goal = lax.rem(my_z + step, depth_z) * depth_x + my_x
        pl.semaphore_signal(barrier, inc=1, device_id=(goal, head), device_id_type=MESH)
    for step in range(1, depth_x):
        goal = my_z * depth_x + lax.rem(my_x + step, depth_x)
        pl.semaphore_signal(barrier, inc=1, device_id=(goal, head), device_id_type=MESH)
    for step in range(1, heads):
        pl.semaphore_signal(
            barrier, inc=1, device_id=(me, lax.rem(head + step, heads)), device_id_type=MESH
        )
    for part in range(group):
        for other in range(heads):
            source = head * group + part

            @pl.when(jnp.logical_or(source != me, head != other))
            def _():
                pl.semaphore_signal(
                    barrier, inc=1, device_id=(source, other), device_id_type=MESH
                )

    self_target = jnp.where(owner == head, 1, 0)
    pl.semaphore_wait(
        barrier, depth_z - 1 + depth_x - 1 + heads - 1 + seq - self_target
    )

    started = []

    def send(source, target, send_sem, recv_sem, device):
        copy = pltpu.make_async_remote_copy(
            src_ref=source,
            dst_ref=target,
            send_sem=send_sem,
            recv_sem=recv_sem,
            device_id=device,
            device_id_type=MESH,
        )
        copy.start()
        started.append(copy)

    def arrived(target, recv_sem):
        pltpu.make_async_copy(target, target, recv_sem).wait()

    for step in range(1, depth_z):
        goal = lax.rem(my_z + step, depth_z) * depth_x + my_x
        send(own_ref, rows_all.at[me], line_send.at[step - 1], rows_recv.at[me], (goal, head))
    own_copy = pltpu.make_async_copy(own_ref, rows_all.at[me], local_sem)
    own_copy.start()
    own_copy.wait()

    def work(block, place):
        def body(index, carry):
            columns = pl.ds(pl.multiple_of(index * tile, tile), tile)
            terms[block, :, columns] = jnp.dot(
                rows_all[block], weight_ref[:, columns], preferred_element_type=jnp.float32
            ).astype(jnp.bfloat16)
            return carry

        lax.fori_loop(0, width // tile, body, 0)
        for turn in range(1, heads):
            other = lax.rem(head + turn, heads)
            start = pl.multiple_of(other * quarter, quarter)
            send(
                terms.at[block, pl.ds(start, quarter)],
                terms_in.at[turn - 1, block],
                term_send.at[place, turn - 1],
                term_recv.at[turn - 1, block],
                (me, other),
            )

    def finish(block):
        start = pl.multiple_of(head * quarter, quarter)
        result = terms[block, pl.ds(start, quarter)].astype(jnp.float32)
        for turn in range(1, heads):
            arrived(terms_in.at[turn - 1, block], term_recv.at[turn - 1, block])
            result += terms_in[turn - 1, block].astype(jnp.float32)
        summed[block] = result.astype(jnp.bfloat16)
        local = jnp.logical_and(block == me, owner == head)

        @pl.when(local)
        def _():
            final_in[slot, head] = summed[block]

        @pl.when(jnp.logical_not(local))
        def _():
            pltpu.make_async_remote_copy(
                src_ref=summed.at[block],
                dst_ref=final_in.at[slot, head],
                send_sem=final_send.at[block],
                recv_sem=final_recv.at[slot, head],
                device_id=(block, owner),
                device_id_type=MESH,
            ).start()

    order = [(i, j) for i in range(depth_z) for j in range(depth_x)]

    def block_of(i, j):
        return lax.rem(my_z + depth_z - i, depth_z) * depth_x + lax.rem(
            my_x + depth_x - j, depth_x
        )

    lag = 2 * depth_x
    for place, (i, j) in enumerate(order):
        block = block_of(i, j)
        if j == 0:
            if i:
                arrived(rows_all.at[block], rows_recv.at[block])
            for step in range(1, depth_x):
                goal = my_z * depth_x + lax.rem(my_x + step, depth_x)
                send(
                    rows_all.at[block],
                    rows_all.at[block],
                    turn_send.at[i, step - 1],
                    rows_recv.at[block],
                    (goal, head),
                )
        else:
            arrived(rows_all.at[block], rows_recv.at[block])
        work(block, place)
        if place >= lag:
            finish(block_of(*order[place - lag]))
    for pair in order[-lag:]:
        finish(block_of(*pair))
    for part in range(group):
        for other in range(heads):
            source = head * group + part

            @pl.when(jnp.logical_or(source != me, head != other))
            def _():
                arrived(final_in.at[part, other], final_recv.at[part, other])

            out_ref[pl.ds(other * quarter, quarter), pl.ds(part * width, width)] = final_in[
                part, other
            ]
    for copy in started:
        copy.wait_send()
    for block in range(seq):

        @pl.when(jnp.logical_not(jnp.logical_and(block == me, owner == head)))
        def _():
            arrived(summed.at[block], final_send.at[block])


def project_outputs(rows_own, weight):
    seq = lax.axis_size("seq")
    heads = lax.axis_size("heads")
    depth_z = 4 if seq % 4 == 0 else seq
    depth_x = seq // depth_z
    group = seq // heads
    rows, depth = rows_own.shape
    width = weight.shape[1]
    quarter = rows // heads
    turns = max(depth_x - 1, 1)
    vmem = pl.BlockSpec(memory_space=pltpu.VMEM)
    dma = pltpu.SemaphoreType.DMA
    return pl.pallas_call(
        functools.partial(output_kernel, depth_z, depth_x, heads),
        out_shape=jax.ShapeDtypeStruct((rows, group * width), jnp.bfloat16),
        in_specs=[vmem] * 2,
        out_specs=vmem,
        scratch_shapes=[
            pltpu.VMEM((seq, rows, depth), jnp.bfloat16),
            pltpu.VMEM((seq, rows, width), jnp.bfloat16),
            pltpu.VMEM((heads - 1, seq, quarter, width), jnp.bfloat16),
            pltpu.VMEM((seq, quarter, width), jnp.bfloat16),
            pltpu.VMEM((group, heads, quarter, width), jnp.bfloat16),
            dma,
            dma((depth_z,)),
            dma((depth_z, turns)),
            dma((seq,)),
            dma((seq, heads - 1)),
            dma((heads - 1, seq)),
            dma((seq,)),
            dma((group, heads)),
        ],
        compiler_params=pltpu.CompilerParams(
            collective_id=1, has_side_effects=True, vmem_limit_bytes=48 * 2**20
        ),
        cost_estimate=pl.CostEstimate(
            flops=2 * rows * seq * depth * width,
            bytes_accessed=400 * 2**20,
            transcendentals=0,
        ),
    )(rows_own, weight)


def layer_norm(values, gain, shift):
    values = values.astype(jnp.float32)
    centre = values - jnp.mean(values, axis=-1, keepdims=True)
    spread = jnp.mean(centre * centre, axis=-1, keepdims=True)
    return centre * lax.rsqrt(spread + 1e-05) * gain + shift


def rms_norm(values, gain):
    values = values.astype(jnp.float32)
    return values * lax.rsqrt(jnp.mean(values * values, axis=-1, keepdims=True) + 1e-06) * gain


def masked_softmax(scores, valid):
    highest = jnp.max(jnp.where(valid, scores, -jnp.inf), axis=-1, keepdims=True)
    raised = jnp.where(valid, jnp.exp(scores - highest), jnp.zeros_like(scores))
    return (raised / jnp.sum(raised, axis=-1, keepdims=True)).astype(jnp.bfloat16)


def shards(
    audio,
    ln_gain,
    ln_shift,
    enc_wq,
    enc_bq,
    enc_wk,
    enc_wv,
    enc_bv,
    enc_wo,
    enc_bo,
    windows,
    dec_wkv,
    dec_bv,
    text,
    norm_gain,
    dec_wq,
    dec_bq,
    dec_wo,
    span_start,
    span_len,
):
    seq_count = lax.axis_size("seq")
    head_count = lax.axis_size("heads")
    seq_index = lax.axis_index("seq")
    head_index = lax.axis_index("heads")
    frames_dev = audio.shape[0]
    enc_width = audio.shape[1]
    heads_dev = windows.shape[0]
    head_size = enc_wq.shape[1] // heads_dev
    all_frames = frames_dev * seq_count
    hidden = layer_norm(audio, ln_gain, ln_shift).astype(jnp.bfloat16)
    enc_query = (jnp.dot(hidden, enc_wq, preferred_element_type=jnp.float32) + enc_bq).astype(
        jnp.bfloat16
    )
    enc_keys = jnp.dot(hidden, enc_wk, preferred_element_type=jnp.float32).astype(jnp.bfloat16)
    enc_values = (jnp.dot(hidden, enc_wv, preferred_element_type=jnp.float32) + enc_bv).astype(
        jnp.bfloat16
    )
    enc_pairs = jnp.stack([enc_keys, enc_values], axis=1)
    widened = with_halo(enc_pairs, (("seq", 0),), EWIN)
    extent = frames_dev + 2 * EWIN
    key_block = widened[:, 0, :].reshape(extent, heads_dev, head_size)
    value_block = widened[:, 1, :].reshape(extent, heads_dev, head_size)
    query_block = enc_query.reshape(frames_dev, heads_dev, head_size)
    scores = jnp.einsum(
        "qhd,khd->hqk", query_block, key_block, preferred_element_type=jnp.float32
    ) * head_size ** (-0.5)
    row_frames = seq_index * frames_dev + jnp.arange(frames_dev, dtype=jnp.int32)
    col_frames = seq_index * frames_dev - EWIN + jnp.arange(extent, dtype=jnp.int32)
    distance = jnp.abs(row_frames[:, None] - col_frames[None, :])
    inside = (col_frames >= 0) & (col_frames < all_frames)
    valid = (distance[None, :, :] <= windows[:, None, None]) & inside[None, None, :]
    enc_weights = masked_softmax(scores, valid)
    enc_context = jnp.einsum(
        "hqk,khd->qhd", enc_weights, value_block, preferred_element_type=jnp.float32
    )
    enc_context = enc_context.astype(jnp.bfloat16).reshape(frames_dev, heads_dev * head_size)
    enc_term = jnp.dot(enc_context, enc_wo, preferred_element_type=jnp.float32)
    share = frames_dev // head_count
    pieces = enc_term.astype(jnp.bfloat16).reshape(head_count, share, enc_width)
    mixed = lax.dynamic_index_in_dim(pieces, head_index, 0, False).astype(jnp.float32)
    for turn in range(1, head_count):
        piece = lax.dynamic_index_in_dim(pieces, (head_index + turn) % head_count, 0, False)
        mixed += lax.ppermute(piece, "heads", shifted(head_count, turn)).astype(jnp.float32)
    own_audio = lax.dynamic_slice_in_dim(audio, head_index * share, share, 0)
    enc_out = (own_audio.astype(jnp.float32) + mixed + enc_bo).astype(jnp.bfloat16)
    groups_dev = dec_wkv.shape[1] // head_count
    pair_width = dec_wkv.shape[2]
    dec_head = pair_width // 2
    band_bias = jnp.concatenate([jnp.zeros_like(dec_bv), dec_bv], axis=1)
    frames_all = jnp.zeros((head_count, share, enc_width), jnp.bfloat16)
    frames_all = lax.dynamic_update_index_in_dim(frames_all, enc_out, head_index, 0)
    for turn in range(1, head_count):
        frames_all = lax.dynamic_update_index_in_dim(
            frames_all,
            lax.ppermute(enc_out, "heads", shifted(head_count, turn)),
            (head_index + head_count - turn) % head_count,
            0,
        )
    frames_all = frames_all.reshape(frames_dev, enc_width)
    weight_group = lax.dynamic_slice_in_dim(
        dec_wkv, head_index * groups_dev, groups_dev, 1
    ).reshape(enc_width, groups_dev * pair_width)
    bias_group = lax.dynamic_slice_in_dim(
        band_bias, head_index * groups_dev, groups_dev, 0
    ).reshape(groups_dev * pair_width)
    band_pairs = (
        jnp.dot(frames_all, weight_group, preferred_element_type=jnp.float32) + bias_group
    ).astype(jnp.bfloat16)
    band_pairs = band_pairs.reshape(frames_dev, groups_dev, pair_width)
    band_wide = with_halo(band_pairs, (("seq", 0),), BAND)
    rows_dev = text.shape[0]
    model_width = text.shape[1]
    query_width = dec_wq.shape[1]
    query_heads = query_width // (groups_dev * dec_head)
    quarter = rows_dev // head_count
    depth = dec_wq.shape[0]
    own_rows = lax.dynamic_slice_in_dim(text, head_index * quarter, quarter, 0)
    normed = rms_norm(own_rows, norm_gain).astype(jnp.bfloat16)
    normed = normed.reshape(quarter, seq_count, depth).transpose(1, 0, 2)
    normed, band_wide = lax.optimization_barrier((normed, band_wide))
    dec_query = project_queries(normed, dec_wq, dec_bq).reshape(
        rows_dev, groups_dev, query_heads, dec_head
    )
    band_extent = band_wide.shape[0]
    band_keys = band_wide[:, :, :dec_head]
    band_values = band_wide[:, :, dec_head:]
    dec_scores = jnp.einsum(
        "rgqd,kgd->rgqk", dec_query, band_keys, preferred_element_type=jnp.float32
    ) * dec_head ** (-0.5)
    band_frames = seq_index * frames_dev - BAND + jnp.arange(band_extent, dtype=jnp.int32)
    in_band = (band_frames[None, :] >= span_start[:, None]) & (
        band_frames[None, :] < (span_start + span_len)[:, None]
    )
    dec_weights = masked_softmax(dec_scores, in_band[:, None, None, :])
    dec_context = jnp.einsum(
        "rgqk,kgd->rgqd", dec_weights, band_values, preferred_element_type=jnp.float32
    )
    dec_context = dec_context.astype(jnp.bfloat16).reshape(rows_dev, query_width)
    summed = project_outputs(dec_context, dec_wo).astype(jnp.float32)
    col_share = model_width // head_count
    own_text = lax.dynamic_slice_in_dim(text, head_index * col_share, col_share, 1)
    dec_out = (own_text.astype(jnp.float32) + summed).astype(jnp.bfloat16)
    return (enc_out, dec_out)


def solution(mesh):
    return jax.shard_map(
        shards,
        mesh=mesh,
        in_specs=(
            P("seq", None),
            P(),
            P(),
            P(None, "heads"),
            P("heads"),
            P(None, "heads"),
            P(None, "heads"),
            P("heads"),
            P("heads", None),
            P(),
            P("heads"),
            P(),
            P(),
            P("seq", None),
            P(),
            P("seq", "heads"),
            P("heads"),
            P("heads", "seq"),
            P("seq"),
            P("seq"),
        ),
        out_specs=(P(("seq", "heads"), None), P("seq", "heads")),
        check_vma=False,
    )
```
